32 devices in a mesh: blocks: 8 (over z, y), filt: 4 (over x, core).
Axes of the slice: x: 2, y: 2, z: 4, core: 2. Of those that a mesh axis runs over, the one named last changes fastest.
Arguments:
- volume: bfloat16 [64, 4, 64, 128], P(None, None, 'blocks'), may hold values from -6 to 6
- w_first: bfloat16 [3, 3, 64, 64], P(None, None, 'filt'), may hold values from -0.25 to 0.25
- w_second: bfloat16 [3, 3, 3, 64, 64], P(None, None, None, 'filt'), may hold values from -0.15625 to 0.15625
- cotangent: bfloat16 [64, 4, 64, 128], P('filt', None, 'blocks'), may hold values from -6 to 6
Outputs:
- output: bfloat16 [64, 4, 64, 128], P('filt', None, 'blocks')
- input_grad: bfloat16 [64, 4, 64, 128], P('filt', None, 'blocks')
- first_grad: float32 [3, 3, 64, 64], P(None, None, 'filt')
- second_grad: float32 [3, 3, 3, 64, 64], P(None, None, None, 'filt')
The draws below stay inside these ranges and needn't reach their ends.
All inputs are finite; a program needn't handle non-finite values.
Results may differ from the reference program's by a relative error of at most 0.012.
Values may be sent and summed in bfloat16 or wider, within the bound.
A program may use at most 64 MiB of HBM per device.

```python
import math
import jax
import jax.numpy as jnp
from jax import lax

C = 64
Z = 4
X = 128
NY = 64


def block_scale(key, shape, cuts, least, top_value):
    def one(axis_at, parts):
        draws = jax.random.uniform(jax.random.fold_in(jax.random.fold_in(key, 6), axis_at), (parts,), jnp.float32, least / len(cuts), top_value / len(cuts))
        return jnp.repeat(jnp.exp(draws), shape[axis_at] // parts).reshape((-1,) + (1,) * (len(shape) - axis_at - 1))

    factor_of = one(*cuts[0])
    for cut in cuts[1:]:
        factor_of = factor_of * one(*cut)
    return factor_of


def noise(own_key, dims, width, reach, shards=(), kind=jnp.bfloat16):
    loudness = block_scale(own_key, dims, shards, -0.22, 0.18) if shards else 1.0
    drawn = jax.random.normal(own_key, dims, jnp.float32) * width * loudness
    return jnp.minimum(jnp.maximum(drawn, -reach), reach).astype(kind)


def setup_inputs(seed: int = 0) -> dict:
    arg_keys = jax.random.split(jax.random.key(seed), 5)
    volume = noise(arg_keys[0], (C, Z, NY, X), 1.0, 6.0, ((2, 8),))
    w_first = noise(arg_keys[1], (3, 3, C, C), (9 * C) ** -0.5, 0.25, ((2, 4),))
    w_second = noise(arg_keys[2], (3, 3, 3, C, C), (27 * C) ** -0.5, 0.15625, ((3, 4),))
    cotangent = noise(arg_keys[3], (C, Z, NY, X), 1.0, 6.0, ((0, 4), (2, 8)))
    return dict(volume=volume, w_first=w_first, w_second=w_second, cotangent=cotangent)


def convolve(field, kernel, dilation, padding):
    result = lax.conv_general_dilated(field[None], kernel, (1, 1, 1), padding, rhs_dilation=dilation, dimension_numbers=('NCDHW', 'DHWOI', 'NCDHW'))
    return result[0]

def first_layer(field, kernel):
    return convolve(field, kernel, (1, 1, 1), ((0, 0), (1, 1), (1, 1)))

def second_layer(field, kernel):
    return convolve(field, kernel, (2, 2, 2), ((2, 2), (2, 2), (2, 2)))

def reference(volume, w_first, w_second, cotangent):
    source = volume.astype(jnp.float32)
    kernel_one = w_first.astype(jnp.float32)[None]
    kernel_two = w_second.astype(jnp.float32)
    pre = first_layer(source, kernel_one)
    hidden = jax.nn.silu(pre).astype(jnp.bfloat16)
    result, pull_two = jax.vjp(second_layer, hidden.astype(jnp.float32), kernel_two)
    output = result.astype(jnp.bfloat16)
    hidden_grad, second_raw = pull_two(cotangent.astype(jnp.float32))
    sigma = jax.nn.sigmoid(pre)
    pre_grad = (hidden_grad * sigma * (1.0 + pre * (1.0 - sigma))).astype(jnp.bfloat16)
    unused, pull_one = jax.vjp(first_layer, source, kernel_one)
    input_raw, first_raw = pull_one(pre_grad.astype(jnp.float32))
    factor = 1.0 / math.sqrt(Z * NY * X)
    return (output, input_raw.astype(jnp.bfloat16), first_raw[0] * factor, second_raw * factor)
```

```python
import functools
import math

import jax
import jax.numpy as jnp
from jax import lax
from jax.experimental import pallas as pl
from jax.experimental.pallas import tpu as pltpu
from jax.sharding import PartitionSpec as P

HALO = 3
MESH = pl.DeviceIdType.MESH


def shifted(row, amount):
    if amount == 0:
        return row
    width = row.shape[1]
    lane = lax.broadcasted_iota(jnp.int32, row.shape, 1)
    moved = pltpu.roll(row, amount % width, 1)
    keep = lane >= amount if amount > 0 else lane < width + amount
    return jnp.where(keep, moved, 0.0)


def rows_of(ref, z, rows, width):
    pieces = []
    start = 0
    while start < len(rows):
        stop = start + 1
        while stop < len(rows) and rows[stop] == rows[stop - 1] + 1:
            stop += 1
        pieces.append(ref[z, :, rows[start] * width : (rows[stop - 1] + 1) * width])
        start = stop
    return pieces[0] if len(pieces) == 1 else jnp.concatenate(pieces, axis=1)


def taps_of(ref, z, row_lists, width):
    return jnp.concatenate([rows_of(ref, z, rows, width) for rows in row_lists], axis=0)


def gather_taps(product, width, channels, count, amounts):
    out = []
    for r in range(count):
        total = None
        for c in range(3):
            part = product[c * channels : (c + 1) * channels, r * width : (r + 1) * width]
            part = shifted(part, amounts[c])
            total = part if total is None else total + part
        out.append(total)
    return out


def dot(a, b):
    return jnp.dot(a, b, preferred_element_type=jnp.float32)


def dot_cells(a, b):
    return lax.dot_general(a, b, (((1,), (1,)), ((), ())), preferred_element_type=jnp.float32)


def kernel(
    sizes,
    vol, cot, w1p, w1g, w2g, w2o,
    out, inp, grads,
    vs, cs, hs, slope, pgs, w1f, w1t, w2f, w2t, part, landed, final, cshift,
    halo_send, halo_recv, fwd_send, fwd_recv, gat_send, gat_recv,
    rs_send, rs_recv, ag_send, ag_recv,
):
    nb, nf, y_rows, width, chunk = sizes
    z_cells, channels, _ = vol.shape
    own = cot.shape[1]
    half = channels // 2
    b = lax.axis_index("blocks")
    f = lax.axis_index("filt")
    mine = pl.ds(pl.multiple_of(f * own, own), own)
    core_half = pl.ds(pl.multiple_of(lax.rem(f, 2) * half, half), half)
    mate = f + 1 - 2 * lax.rem(f, 2)

    barrier = pltpu.get_barrier_semaphore()
    for d in range(1, nf):
        pl.semaphore_signal(barrier, 1, device_id=(b, lax.rem(f + d, nf)), device_id_type=MESH)
    for d in range(1, nb):
        pl.semaphore_signal(barrier, 1, device_id=(lax.rem(b + d, nb), f), device_id_type=MESH)
    pl.semaphore_wait(barrier, nf - 1 + nb - 1)

    hw = HALO * width
    body = y_rows * width
    low, mid, high = slice(0, hw), slice(hw, hw + body), slice(hw + body, 2 * hw + body)
    has_low, has_high = b > 0, b < nb - 1
    lands = (low, high)
    gives = (slice(body - hw, body), slice(0, hw))
    sends_if = (has_high, has_low)
    lands_if = (has_low, has_high)
    targets = (b + 1, b - 1)

    def remote(src, dst, send, recv, device):
        return pltpu.make_async_remote_copy(
            src_ref=src, dst_ref=dst, send_sem=send, recv_sem=recv, device_id=device, device_id_type=MESH
        )

    def halo(side):
        return (
            remote(vol.at[:, core_half, gives[side]], vs.at[:, core_half, lands[side]],
                   halo_send.at[side], halo_recv.at[side], (targets[side], f)),
            remote(cot.at[:, :, gives[side]], cs.at[:, mine, lands[side]],
                   halo_send.at[2 + side], halo_recv.at[2 + side], (targets[side], f)),
        )

    def forward_volume(side):
        ref = vs.at[:, core_half, lands[side]]
        return remote(ref, ref, fwd_send.at[side], fwd_recv.at[side], (b, mate))

    def forward_cot(side, d):
        ref = cs.at[:, mine, lands[side]]
        slot = 2 * d + side
        return remote(ref, ref, fwd_send.at[slot], fwd_recv.at[slot], (b, lax.rem(f + d, nf)))

    def gathers(d):
        to = lax.rem(f + d, nf)
        device = (b, to)
        pairs = (
            (w1p, w1f.at[:, mine, :]),
            (cot, cs.at[:, mine, mid]),
            (w2g, w2f.at[:, :, mine, :]),
            (w1g.at[to], w1t.at[:, mine, :]),
        )
        return [
            remote(s, t, gat_send.at[4 * d + k], gat_recv.at[4 * d + k], device)
            for k, (s, t) in enumerate(pairs)
        ]

    for side in (0, 1):
        @pl.when(sends_if[side])
        def _():
            for copy in halo(side):
                copy.start()
    gathered = [gathers(d) for d in range(1, nf)]
    for k in range(4):
        for copies in gathered:
            copies[k].start()

    vs[:, :, mid] = vol[...]
    cs[:, mine, mid] = cot[...]
    w1f[:, mine, :] = w1p[...]
    w2f[:, :, mine, :] = w2g[...]
    w1t[:, mine, :] = w1g[f]
    for side in (0, 1):
        @pl.when(jnp.logical_not(lands_if[side]))
        def _():
            vs[:, :, lands[side]] = jnp.zeros((z_cells, channels, hw), vs.dtype)
            cs[:, :, lands[side]] = jnp.zeros((z_cells, channels, hw), cs.dtype)
    for z in range(z_cells):
        for y in range(y_rows):
            at = slice(y * width, (y + 1) * width)
            row = cot[z, :, at].astype(jnp.float32)
            for c in range(3):
                cshift[z, c * own : (c + 1) * own, at] = shifted(row, 2 * (c - 1)).astype(cshift.dtype)

    for copies in gathered:
        copies[0].wait_recv()
    first_weight = w1f[...].reshape(3 * channels, w1f.shape[2])

    def first_layer(rows):
        for z in range(z_cells):
            product = dot(
                first_weight,
                taps_of(vs, z, [[y + t - 1 + HALO for y in rows] for t in range(3)], width),
            )
            for y, pre in zip(rows, gather_taps(product, width, channels, len(rows), (1, 0, -1))):
                at = slice((y + 2) * width, (y + 3) * width)
                sigma = 1.0 / (1.0 + jnp.exp(-pre))
                hs[z, :, at] = (pre * sigma).astype(hs.dtype)
                slope[z, :, at] = sigma * (1.0 + pre * (1.0 - sigma))

    inner = list(range(1, y_rows - 1))
    outer = [-2, -1, 0, y_rows - 1, y_rows, y_rows + 1]
    for k in range(0, len(inner), 2):
        first_layer(inner[k : k + 2])

    for side in (0, 1):
        @pl.when(lands_if[side])
        def _():
            volume_copy, cot_copy = halo(side)
            volume_copy.wait_recv()
            forward_volume(side).start()
            cot_copy.wait_recv()
            for d in range(1, nf):
                forward_cot(side, d).start()

    for copies in gathered:
        copies[1].wait_recv()
        copies[2].wait_recv()
    for a in range(3):
        w2t[a] = jnp.transpose(w2f[a].reshape(3 * channels, w2f.shape[3]))

    def hidden_grad(rows):
        for z in range(z_cells):
            product = None
            for a in range(3):
                at_z = z - 2 * (a - 1)
                if 0 <= at_z < z_cells:
                    term = dot(
                        w2t[a],
                        taps_of(cs, at_z, [[y - 2 * (t - 1) + HALO for y in rows] for t in range(3)], width),
                    )
                    product = term if product is None else product + term
            for y, value in zip(rows, gather_taps(product, width, channels, len(rows), (-2, 0, 2))):
                grad = value * slope[z, :, (y + 2) * width : (y + 3) * width]
                pgs[z, :, (y + 1) * width : (y + 2) * width] = grad.astype(pgs.dtype)

    inner_grad = list(range(2, y_rows - 2))
    outer_grad = [y for y in range(-1, y_rows + 1) if y not in inner_grad]
    for k in range(0, len(inner_grad), 2):
        hidden_grad(inner_grad[k : k + 2])

    for side in (0, 1):
        @pl.when(lands_if[side])
        def _():
            forward_volume(side).wait_recv()
    for k in range(0, len(outer), 2):
        first_layer(outer[k : k + 2])
    for side, at in ((0, slice(0, 2 * width)), (1, slice((y_rows + 2) * width, (y_rows + 4) * width))):
        @pl.when(jnp.logical_not(lands_if[side]))
        def _():
            hs[:, :, at] = jnp.zeros((z_cells, channels, 2 * width), hs.dtype)

    def hidden_taps(z, rows):
        return taps_of(hs, z, [[y + 2 * t for y in rows] for t in range(3)], width)

    factor = 1.0 / math.sqrt(z_cells * y_rows * nb * width)
    every = list(range(y_rows))
    for a in range(3):
        total = None
        for z in range(z_cells):
            at_z = z + 2 * (a - 1)
            if 0 <= at_z < z_cells:
                term = dot_cells(cshift[z], hidden_taps(at_z, every))
                total = term if total is None else total + term
        if total is None:
            total = jnp.zeros((3 * own, 3 * channels), jnp.float32)
        part[a * 3 * own : (a + 1) * 3 * own, :] = total * factor

    for side in (0, 1):
        @pl.when(lands_if[side])
        def _():
            for d in range(1, nf):
                forward_cot(side, d).wait_recv()
    for k in range(0, len(outer_grad), 2):
        hidden_grad(outer_grad[k : k + 2])
    for side, at in ((0, slice(0, width)), (1, slice((y_rows + 1) * width, (y_rows + 2) * width))):
        @pl.when(jnp.logical_not(lands_if[side]))
        def _():
            pgs[:, :, at] = jnp.zeros((z_cells, channels, width), pgs.dtype)

    total = None
    for z in range(z_cells):
        columns = []
        for y in range(y_rows):
            row = pgs[z, mine, (y + 1) * width : (y + 2) * width].astype(jnp.float32)
            columns.append(
                jnp.concatenate([shifted(row, c - 1).astype(pgs.dtype) for c in range(3)], axis=0)
            )
        term = dot_cells(
            jnp.concatenate(columns, axis=1),
            taps_of(vs, z, [[y + t - 1 + HALO for y in every] for t in range(3)], width),
        )
        total = term if total is None else total + term
    used = 12 * own
    part[9 * own : used, :] = total * factor
    if part.shape[0] > used:
        part[used:, :] = jnp.zeros((part.shape[0] - used, part.shape[1]), part.dtype)

    def piece(index):
        return pl.ds(pl.multiple_of(index * chunk, 8), chunk)

    scatters = []
    for d in range(1, nb):
        to = lax.rem(b + d, nb)
        copy = remote(part.at[piece(to), :], landed.at[d], rs_send.at[d], rs_recv.at[d], (to, f))
        copy.start()
        scatters.append(copy)

    for z in range(z_cells):
        for k in range(0, y_rows, 2):
            product = None
            for a in range(3):
                at_z = z + 2 * (a - 1)
                if 0 <= at_z < z_cells:
                    term = dot(w2o[a], hidden_taps(at_z, every[k : k + 2]))
                    product = term if product is None else product + term
            for y, value in zip(every[k : k + 2], gather_taps(product, width, own, 2, (2, 0, -2))):
                out[z, :, y * width : (y + 1) * width] = value.astype(out.dtype)

    total = part[piece(b), :]
    for d in range(1, nb):
        scatters[d - 1].wait_recv()
        total = total + landed[d]
    final[piece(b), :] = total
    spreads = []
    for d in range(1, nb):
        to = lax.rem(b + d, nb)
        ref = final.at[piece(b), :]
        copy = remote(ref, ref, ag_send.at[d], ag_recv.at[d], (to, f))
        copy.start()
        spreads.append(copy)

    for copies in gathered:
        copies[3].wait_recv()
    back_weight = jnp.transpose(w1t[...].reshape(3 * channels, w1t.shape[2]))
    for z in range(z_cells):
        for k in range(0, y_rows, 2):
            rows = every[k : k + 2]
            product = dot(back_weight, taps_of(pgs, z, [[y + 2 - t for y in rows] for t in range(3)], width))
            for y, value in zip(rows, gather_taps(product, width, own, 2, (-1, 0, 1))):
                inp[z, :, y * width : (y + 1) * width] = value.astype(inp.dtype)

    for copy in spreads:
        copy.wait_recv()
    grads[...] = final[:used, :]

    for side in (0, 1):
        @pl.when(sends_if[side])
        def _():
            for copy in halo(side):
                copy.wait_send()

        @pl.when(lands_if[side])
        def _():
            forward_volume(side).wait_send()
            for d in range(1, nf):
                forward_cot(side, d).wait_send()
    for copies in gathered:
        for copy in copies:
            copy.wait_send()
    for copy in scatters + spreads:
        copy.wait_send()


def per_device(nb, nf, volume, w_first, w_second, cotangent):
    channels, z_cells, y_rows, width = volume.shape
    own = cotangent.shape[0]
    cells = y_rows * width
    vol = volume.transpose(1, 0, 2, 3).reshape(z_cells, channels, cells)
    cot = cotangent.transpose(1, 0, 2, 3).reshape(z_cells, own, cells)
    w1p = w_first.transpose(1, 2, 0, 3).reshape(3, own, 3 * channels)
    w1g = w_first.reshape(3, 3, own, nf, own).transpose(3, 0, 2, 1, 4).reshape(nf, 3, own, 3 * own)
    w2g = w_second.transpose(0, 1, 3, 2, 4).reshape(3, 3, own, 3 * channels)
    w2o = w_second.transpose(0, 2, 3, 1, 4).reshape(3, 3 * own, 3 * channels)
    used = 12 * own
    chunk = -(-used // (8 * nb)) * 8
    wide = (y_rows + 2 * HALO) * width
    bf16, f32 = jnp.bfloat16, jnp.float32
    dma = pltpu.SemaphoreType.DMA
    out, inp, grads = pl.pallas_call(
        functools.partial(kernel, (nb, nf, y_rows, width, chunk)),
        out_shape=(
            jax.ShapeDtypeStruct((z_cells, own, cells), bf16),
            jax.ShapeDtypeStruct((z_cells, own, cells), bf16),
            jax.ShapeDtypeStruct((used, 3 * channels), f32),
        ),
        in_specs=[pl.BlockSpec(memory_space=pltpu.VMEM)] * 6,
        out_specs=(pl.BlockSpec(memory_space=pltpu.VMEM),) * 3,
        scratch_shapes=[
            pltpu.VMEM((z_cells, channels, wide), bf16),
            pltpu.VMEM((z_cells, channels, wide), bf16),
            pltpu.VMEM((z_cells, channels, (y_rows + 4) * width), bf16),
            pltpu.VMEM((z_cells, channels, (y_rows + 4) * width), f32),
            pltpu.VMEM((z_cells, channels, (y_rows + 2) * width), bf16),
            pltpu.VMEM((3, channels, 3 * channels), bf16),
            pltpu.VMEM((3, channels, 3 * own), bf16),
            pltpu.VMEM((3, 3, channels, 3 * channels), bf16),
            pltpu.VMEM((3, 3 * channels, 3 * channels), bf16),
            pltpu.VMEM((nb * chunk, 3 * channels), f32),
            pltpu.VMEM((nb, chunk, 3 * channels), f32),
            pltpu.VMEM((nb * chunk, 3 * channels), f32),
            pltpu.VMEM((z_cells, 3 * own, cells), bf16),
            dma((4,)), dma((4,)),
            dma((2 * nf,)), dma((2 * nf,)),
            dma((4 * nf,)), dma((4 * nf,)),
            dma((nb,)), dma((nb,)), dma((nb,)), dma((nb,)),
        ],
        compiler_params=pltpu.CompilerParams(
            collective_id=0, has_side_effects=True, vmem_limit_bytes=40 * 1024 * 1024
        ),
    )(vol, cot, w1p, w1g, w2g, w2o)
    output = out.reshape(z_cells, own, y_rows, width).transpose(1, 0, 2, 3)
    input_grad = inp.reshape(z_cells, own, y_rows, width).transpose(1, 0, 2, 3)
    second = grads[: 9 * own].reshape(3, 3, own, 3, channels).transpose(0, 3, 1, 2, 4)
    first = grads[9 * own :].reshape(3, own, 3, channels).transpose(2, 0, 1, 3)
    return (output, input_grad, first, second)


def solution(mesh):
    return jax.shard_map(
        functools.partial(per_device, mesh.shape["blocks"], mesh.shape["filt"]),
        mesh=mesh,
        in_specs=(
            P(None, None, "blocks", None),
            P(None, None, "filt", None),
            P(None, None, None, "filt", None),
            P("filt", None, "blocks", None),
        ),
        out_specs=(
            P("filt", None, "blocks", None),
            P("filt", None, "blocks", None),
            P(None, None, "filt", None),
            P(None, None, None, "filt", None),
        ),
        check_vma=False,
    )
```

```python
import functools
import math

import jax
import jax.numpy as jnp
from jax import lax
from jax.experimental import pallas as pl
from jax.experimental.pallas import tpu as pltpu
from jax.sharding import PartitionSpec as P

HALO = 3
MESH = pl.DeviceIdType.MESH


def shifted(row, amount):
    if amount == 0:
        return row
    width = row.shape[1]
    lane = lax.broadcasted_iota(jnp.int32, row.shape, 1)
    moved = pltpu.roll(row, amount % width, 1)
    keep = lane >= amount if amount > 0 else lane < width + amount
    return jnp.where(keep, moved, 0.0)


def rows_of(ref, z, rows, width):
    pieces = []
    start = 0
    while start < len(rows):
        stop = start + 1
        while stop < len(rows) and rows[stop] == rows[stop - 1] + 1:
            stop += 1
        pieces.append(ref[z, :, rows[start] * width : (rows[stop - 1] + 1) * width])
        start = stop
    return pieces[0] if len(pieces) == 1 else jnp.concatenate(pieces, axis=1)


def taps_of(ref, z, row_lists, width):
    return jnp.concatenate([rows_of(ref, z, rows, width) for rows in row_lists], axis=0)


def gather_taps(product, width, channels, count, amounts):
    out = []
    for r in range(count):
        total = None
        for c in range(3):
            part = product[c * channels : (c + 1) * channels, r * width : (r + 1) * width]
            part = shifted(part, amounts[c])
            total = part if total is None else total + part
        out.append(total)
    return out


def dot(a, b):
    return jnp.dot(a, b, preferred_element_type=jnp.float32)


def dot_cells(a, b):
    return lax.dot_general(a, b, (((1,), (1,)), ((), ())), preferred_element_type=jnp.float32)


def packed(blocks, lanes):
    tiles = [block[:, :lanes] for block in blocks]
    last = [block[:, lanes:] for block in blocks]
    if len(last) % 2:
        last.append(jnp.zeros_like(last[0]))
    tiles += [jnp.concatenate(last[k : k + 2], axis=1) for k in range(0, len(last), 2)]
    return tiles


def unpacked(tiles, count, channels, index, tap):
    if tap < 2:
        tile = tiles[index]
        return tile[:, tap * channels : (tap + 1) * channels]
    tile = tiles[count + index // 2]
    side = index % 2
    return tile[:, side * channels : (side + 1) * channels]


def kernel(
    sizes,
    vol, cot, w1p, w2g, w2o,
    out, inp, first_out, second_out,
    vs, cs, hs, slope, pgs, w1f, w1t, w2f, w2t, cshift,
    part1, landed1, final1, part2, landed2, final2,
    halo_send, halo_recv, fwd_send, fwd_recv, vfwd_send, vfwd_recv, gat_send, gat_recv,
    rs_send, rs_recv, ag_send, ag_recv,
):
    nb, nf, y_rows, width = sizes
    z_cells, channels, _ = vol.shape
    own = cot.shape[1]
    half = channels // 2
    b = lax.axis_index("blocks")
    f = lax.axis_index("filt")
    mine = pl.ds(pl.multiple_of(f * own, own), own)
    core_half = pl.ds(pl.multiple_of(lax.rem(f, 2) * half, half), half)
    mate = f + 1 - 2 * lax.rem(f, 2)
    across = lax.rem(f + 2, nf)
    theirs = pl.ds(pl.multiple_of(across * own, own), own)

    barrier = pltpu.get_barrier_semaphore()
    for d in range(1, nf):
        pl.semaphore_signal(barrier, 1, device_id=(b, lax.rem(f + d, nf)), device_id_type=MESH)
    for d in range(1, nb):
        pl.semaphore_signal(barrier, 1, device_id=(lax.rem(b + d, nb), f), device_id_type=MESH)
    pl.semaphore_wait(barrier, nf - 1 + nb - 1)

    hw = HALO * width
    body = y_rows * width
    low, mid, high = slice(0, hw), slice(hw, hw + body), slice(hw + body, 2 * hw + body)
    has_low, has_high = b > 0, b < nb - 1
    lands = (low, high)
    gives = (slice(body - hw, body), slice(0, hw))
    sends_if = (has_high, has_low)
    lands_if = (has_low, has_high)
    targets = (b + 1, b - 1)

    def remote(src, dst, send, recv, device):
        return pltpu.make_async_remote_copy(
            src_ref=src, dst_ref=dst, send_sem=send, recv_sem=recv, device_id=device, device_id_type=MESH
        )

    def halo(side):
        return (
            remote(vol.at[:, core_half, gives[side]], vs.at[:, core_half, lands[side]],
                   halo_send.at[side], halo_recv.at[side], (targets[side], f)),
            remote(cot.at[:, :, gives[side]], cs.at[:, mine, lands[side]],
                   halo_send.at[2 + side], halo_recv.at[2 + side], (targets[side], f)),
        )

    def forward_volume(side):
        ref = vs.at[:, core_half, lands[side]]
        return remote(ref, ref, vfwd_send.at[side], vfwd_recv.at[side], (b, mate))

    roles = ((mate, mine), (across, mine), (mate, theirs))

    def forward_cot(side, role):
        to, block = roles[role]
        ref = cs.at[:, block, lands[side]]
        slot = 2 * role + side
        return remote(ref, ref, fwd_send.at[slot], fwd_recv.at[slot], (b, to))

    def gather(k, role):
        to, block = roles[role]
        source = (w1p, cot, w2g)[k]
        ref = (w1f.at[:, block, :], cs.at[:, block, mid], w2f.at[:, :, block, :])[k]
        if role == 2:
            source = ref
        slot = 3 * role + k
        return remote(source, ref, gat_send.at[slot], gat_recv.at[slot], (b, to))

    for role in (1, 0):
        gather(0, role).start()
    for side in (0, 1):
        @pl.when(sends_if[side])
        def _():
            volume_copy, cot_copy = halo(side)
            cot_copy.start()
            volume_copy.start()
    for k in (1, 2):
        for role in (1, 0):
            gather(k, role).start()

    vs[:, :, mid] = vol[...]
    cs[:, mine, mid] = cot[...]
    w1f[:, mine, :] = w1p[...]
    w2f[:, :, mine, :] = w2g[...]
    for side in (0, 1):
        @pl.when(jnp.logical_not(lands_if[side]))
        def _():
            vs[:, :, lands[side]] = jnp.zeros((z_cells, channels, hw), vs.dtype)
            cs[:, :, lands[side]] = jnp.zeros((z_cells, channels, hw), cs.dtype)
    for z in range(z_cells):
        for y in range(y_rows):
            at = slice(y * width, (y + 1) * width)
            row = cot[z, :, at].astype(jnp.float32)
            for c in range(3):
                cshift[z, c * own : (c + 1) * own, at] = shifted(row, 2 * (c - 1)).astype(cshift.dtype)

    def pass_on(k):
        gather(k, 1).wait_recv()
        gather(k, 2).start()

    def complete(k):
        gather(k, 0).wait_recv()
        gather(k, 2).wait_recv()

    pass_on(0)
    complete(0)
    first_weight = w1f[...].reshape(3 * channels, w1f.shape[2])

    def first_layer(rows):
        for z in range(z_cells):
            product = dot(
                first_weight,
                taps_of(vs, z, [[y + t - 1 + HALO for y in rows] for t in range(3)], width),
            )
            for y, pre in zip(rows, gather_taps(product, width, channels, len(rows), (1, 0, -1))):
                at = slice((y + 2) * width, (y + 3) * width)
                sigma = 1.0 / (1.0 + jnp.exp(-pre))
                hs[z, :, at] = (pre * sigma).astype(hs.dtype)
                slope[z, :, at] = sigma * (1.0 + pre * (1.0 - sigma))

    inner = list(range(1, y_rows - 1))
    outer = [-2, -1, 0, y_rows - 1, y_rows, y_rows + 1]
    chunks = [inner[k : k + 2] for k in range(0, len(inner), 2)]
    first_layer(chunks[0])
    pass_on(1)
    for rows in chunks[1:2]:
        first_layer(rows)
    for side in (0, 1):
        @pl.when(lands_if[side])
        def _():
            volume_copy, cot_copy = halo(side)
            cot_copy.wait_recv()
            forward_cot(side, 1).start()
            forward_cot(side, 0).start()
    for rows in chunks[2:]:
        first_layer(rows)
    pass_on(2)
    for side in (0, 1):
        @pl.when(lands_if[side])
        def _():
            halo(side)[0].wait_recv()
            forward_volume(side).start()

    for c in range(3):
        w1t[c] = jnp.transpose(w1f[c])
    complete(1)
    complete(2)
    for a in range(3):
        w2t[a] = jnp.transpose(w2f[a].reshape(3 * channels, w2f.shape[3]))

    def hidden_grad(rows):
        for z in range(z_cells):
            product = None
            for a in range(3):
                at_z = z - 2 * (a - 1)
                if 0 <= at_z < z_cells:
                    term = dot(
                        w2t[a],
                        taps_of(cs, at_z, [[y - 2 * (t - 1) + HALO for y in rows] for t in range(3)], width),
                    )
                    product = term if product is None else product + term
            for y, value in zip(rows, gather_taps(product, width, channels, len(rows), (-2, 0, 2))):
                grad = value * slope[z, :, (y + 2) * width : (y + 3) * width]
                pgs[z, :, (y + 1) * width : (y + 2) * width] = grad.astype(pgs.dtype)

    inner_grad = list(range(2, y_rows - 2))
    outer_grad = [y for y in range(-1, y_rows + 1) if y not in inner_grad]
    for k in range(0, len(inner_grad), 2):
        hidden_grad(inner_grad[k : k + 2])

    for side in (0, 1):
        @pl.when(lands_if[side])
        def _():
            forward_volume(side).wait_recv()
            forward_cot(side, 1).wait_recv()
            forward_cot(side, 2).start()
    for k in range(0, len(outer), 2):
        first_layer(outer[k : k + 2])
    for side, at in ((0, slice(0, 2 * width)), (1, slice((y_rows + 2) * width, (y_rows + 4) * width))):
        @pl.when(jnp.logical_not(lands_if[side]))
        def _():
            hs[:, :, at] = jnp.zeros((z_cells, channels, 2 * width), hs.dtype)

    def hidden_taps(z, rows):
        return taps_of(hs, z, [[y + 2 * t for y in rows] for t in range(3)], width)

    factor = 1.0 / math.sqrt(z_cells * y_rows * nb * width)
    every = list(range(y_rows))
    lanes = 2 * channels

    def reduction(which, part, landed, final):
        chunk = part.shape[0] // nb

        def piece(index):
            return pl.ds(index * chunk, chunk)

        def scatter(d):
            to = lax.rem(b + d, nb)
            slot = which * nb + d
            return remote(part.at[piece(to)], landed.at[d], rs_send.at[slot], rs_recv.at[slot], (to, f))

        def spread(d):
            ref = final.at[piece(b)]
            slot = which * nb + d
            return remote(ref, ref, ag_send.at[slot], ag_recv.at[slot], (lax.rem(b + d, nb), f))

        def fill(blocks):
            tiles = packed(blocks, lanes)
            for k, tile in enumerate(tiles):
                part[k] = (tile * factor).astype(part.dtype)
            for k in range(len(tiles), part.shape[0]):
                part[k] = jnp.zeros(part.shape[1:], part.dtype)
            for d in range(1, nb):
                scatter(d).start()

        def turn():
            total = part[piece(b)].astype(jnp.float32)
            for d in range(1, nb):
                scatter(d).wait_recv()
                total = total + landed[d].astype(jnp.float32)
            final[piece(b)] = total.astype(final.dtype)
            for d in range(1, nb):
                spread(d).start()

        def finish():
            for d in range(1, nb):
                spread(d).wait_recv()

        def drain():
            for d in range(1, nb):
                scatter(d).wait_send()
                spread(d).wait_send()

        return fill, turn, finish, drain

    first_sum = reduction(0, part1, landed1, final1)
    second_sum = reduction(1, part2, landed2, final2)

    blocks = []
    for a in range(3):
        total = None
        for z in range(z_cells):
            at_z = z + 2 * (a - 1)
            if 0 <= at_z < z_cells:
                term = dot_cells(cshift[z], hidden_taps(at_z, every))
                total = term if total is None else total + term
        if total is None:
            total = jnp.zeros((3 * own, 3 * channels), jnp.float32)
        blocks += [total[c * own : (c + 1) * own] for c in range(3)]
    second_sum[0](blocks)

    for side in (0, 1):
        @pl.when(lands_if[side])
        def _():
            forward_cot(side, 0).wait_recv()
            forward_cot(side, 2).wait_recv()
    for k in range(0, len(outer_grad), 2):
        hidden_grad(outer_grad[k : k + 2])
    for side, at in ((0, slice(0, width)), (1, slice((y_rows + 1) * width, (y_rows + 2) * width))):
        @pl.when(jnp.logical_not(lands_if[side]))
        def _():
            pgs[:, :, at] = jnp.zeros((z_cells, channels, width), pgs.dtype)

    total = None
    for z in range(z_cells):
        columns = []
        for y in range(y_rows):
            row = pgs[z, mine, (y + 1) * width : (y + 2) * width].astype(jnp.float32)
            columns.append(
                jnp.concatenate([shifted(row, c - 1).astype(pgs.dtype) for c in range(3)], axis=0)
            )
        term = dot_cells(
            jnp.concatenate(columns, axis=1),
            taps_of(vs, z, [[y + t - 1 + HALO for y in every] for t in range(3)], width),
        )
        total = term if total is None else total + term
    first_sum[0]([total[c * own : (c + 1) * own] for c in range(3)])
    second_sum[1]()

    for z in range(z_cells):
        for k in range(0, y_rows, 2):
            product = None
            for a in range(3):
                at_z = z + 2 * (a - 1)
                if 0 <= at_z < z_cells:
                    term = dot(w2o[a], hidden_taps(at_z, every[k : k + 2]))
                    product = term if product is None else product + term
            for y, value in zip(every[k : k + 2], gather_taps(product, width, own, 2, (2, 0, -2))):
                out[z, :, y * width : (y + 1) * width] = value.astype(out.dtype)

    first_sum[1]()

    back_weight = jnp.concatenate(
        [
            jnp.concatenate(
                [w1t[c, pl.ds(pl.multiple_of(t * channels + f * own, own), own), :] for t in range(3)], axis=1
            )
            for c in range(3)
        ],
        axis=0,
    )
    for z in range(z_cells):
        for k in range(0, y_rows, 2):
            rows = every[k : k + 2]
            product = dot(back_weight, taps_of(pgs, z, [[y + 2 - t for y in rows] for t in range(3)], width))
            for y, value in zip(rows, gather_taps(product, width, own, 2, (-1, 0, 1))):
                inp[z, :, y * width : (y + 1) * width] = value.astype(inp.dtype)

    second_sum[2]()
    tiles = [final2[k].astype(jnp.float32) for k in range(14)]
    for a in range(3):
        for t in range(3):
            for c in range(3):
                second_out[a, t, c] = unpacked(tiles, 9, channels, 3 * a + c, t)
    first_sum[2]()
    tiles = [final1[k].astype(jnp.float32) for k in range(5)]
    for t in range(3):
        for c in range(3):
            first_out[t, c] = unpacked(tiles, 3, channels, c, t)

    for side in (0, 1):
        @pl.when(sends_if[side])
        def _():
            for copy in halo(side):
                copy.wait_send()

        @pl.when(lands_if[side])
        def _():
            forward_volume(side).wait_send()
            for role in range(3):
                forward_cot(side, role).wait_send()
    for role in range(3):
        for k in range(3):
            gather(k, role).wait_send()
    first_sum[3]()
    second_sum[3]()


def per_device(nb, nf, volume, w_first, w_second, cotangent):
    channels, z_cells, y_rows, width = volume.shape
    own = cotangent.shape[0]
    cells = y_rows * width
    vol = volume.transpose(1, 0, 2, 3).reshape(z_cells, channels, cells)
    cot = cotangent.transpose(1, 0, 2, 3).reshape(z_cells, own, cells)
    w1p = w_first.transpose(1, 2, 0, 3).reshape(3, own, 3 * channels)
    w2g = w_second.transpose(0, 1, 3, 2, 4).reshape(3, 3, own, 3 * channels)
    w2o = w_second.transpose(0, 2, 3, 1, 4).reshape(3, 3 * own, 3 * channels)
    tiles1, tiles2 = (-(-count // nb) * nb for count in (5, 14))
    tile = (own, 2 * channels)
    wide = (y_rows + 2 * HALO) * width
    bf16, f32 = jnp.bfloat16, jnp.float32
    dma = pltpu.SemaphoreType.DMA
    out, inp, first, second = pl.pallas_call(
        functools.partial(kernel, (nb, nf, y_rows, width)),
        out_shape=(
            jax.ShapeDtypeStruct((z_cells, own, cells), bf16),
            jax.ShapeDtypeStruct((z_cells, own, cells), bf16),
            jax.ShapeDtypeStruct((3, 3, own, channels), f32),
            jax.ShapeDtypeStruct((3, 3, 3, own, channels), f32),
        ),
        in_specs=[pl.BlockSpec(memory_space=pltpu.VMEM)] * 5,
        out_specs=(pl.BlockSpec(memory_space=pltpu.VMEM),) * 4,
        scratch_shapes=[
            pltpu.VMEM((z_cells, channels, wide), bf16),
            pltpu.VMEM((z_cells, channels, wide), bf16),
            pltpu.VMEM((z_cells, channels, (y_rows + 4) * width), bf16),
            pltpu.VMEM((z_cells, channels, (y_rows + 4) * width), f32),
            pltpu.VMEM((z_cells, channels, (y_rows + 2) * width), bf16),
            pltpu.VMEM((3, channels, 3 * channels), bf16),
            pltpu.VMEM((3, 3 * channels, channels), bf16),
            pltpu.VMEM((3, 3, channels, 3 * channels), bf16),
            pltpu.VMEM((3, 3 * channels, 3 * channels), bf16),
            pltpu.VMEM((z_cells, 3 * own, cells), bf16),
            pltpu.VMEM((tiles1,) + tile, bf16),
            pltpu.VMEM((nb, tiles1 // nb) + tile, bf16),
            pltpu.VMEM((tiles1,) + tile, bf16),
            pltpu.VMEM((tiles2,) + tile, bf16),
            pltpu.VMEM((nb, tiles2 // nb) + tile, bf16),
            pltpu.VMEM((tiles2,) + tile, bf16),
            dma((4,)), dma((4,)), dma((6,)), dma((6,)), dma((2,)), dma((2,)), dma((9,)), dma((9,)),
            dma((2 * nb,)), dma((2 * nb,)), dma((2 * nb,)), dma((2 * nb,)),
        ],
        compiler_params=pltpu.CompilerParams(
            collective_id=0, has_side_effects=True, vmem_limit_bytes=40 * 1024 * 1024
        ),
    )(vol, cot, w1p, w2g, w2o)
    output = out.reshape(z_cells, own, y_rows, width).transpose(1, 0, 2, 3)
    input_grad = inp.reshape(z_cells, own, y_rows, width).transpose(1, 0, 2, 3)
    return (output, input_grad, first, second)


def solution(mesh):
    return jax.shard_map(
        functools.partial(per_device, mesh.shape["blocks"], mesh.shape["filt"]),
        mesh=mesh,
        in_specs=(
            P(None, None, "blocks", None),
            P(None, None, "filt", None),
            P(None, None, None, "filt", None),
            P("filt", None, "blocks", None),
        ),
        out_specs=(
            P("filt", None, "blocks", None),
            P("filt", None, "blocks", None),
            P(None, None, "filt", None),
            P(None, None, None, "filt", None),
        ),
        check_vma=False,
    )
```

```python
import functools
import math

import jax
import jax.numpy as jnp
from jax import lax
from jax.experimental import pallas as pl
from jax.experimental.pallas import tpu as pltpu
from jax.sharding import PartitionSpec as P

HALO = 3
MESH = pl.DeviceIdType.MESH


def shifted(row, amount):
    if amount == 0:
        return row
    width = row.shape[1]
    lane = lax.broadcasted_iota(jnp.int32, row.shape, 1)
    moved = pltpu.roll(row, amount % width, 1)
    keep = lane >= amount if amount > 0 else lane < width + amount
    return jnp.where(keep, moved, 0.0)


def rows_of(ref, z, rows, width):
    pieces = []
    start = 0
    while start < len(rows):
        stop = start + 1
        while stop < len(rows) and rows[stop] == rows[stop - 1] + 1:
            stop += 1
        pieces.append(ref[z, :, rows[start] * width : (rows[stop - 1] + 1) * width])
        start = stop
    return pieces[0] if len(pieces) == 1 else jnp.concatenate(pieces, axis=1)


def taps_of(ref, z, row_lists, width):
    return jnp.concatenate([rows_of(ref, z, rows, width) for rows in row_lists], axis=0)


def gather_taps(product, width, channels, count, amounts):
    out = []
    for r in range(count):
        total = None
        for c in range(3):
            part = product[c * channels : (c + 1) * channels, r * width : (r + 1) * width]
            part = shifted(part, amounts[c])
            total = part if total is None else total + part
        out.append(total)
    return out


def dot(a, b):
    return jnp.dot(a, b, preferred_element_type=jnp.float32)


def dot_cells(a, b):
    return lax.dot_general(a, b, (((1,), (1,)), ((), ())), preferred_element_type=jnp.float32)


def packed(blocks, lanes):
    tiles = [block[:, :lanes] for block in blocks]
    last = [block[:, lanes:] for block in blocks]
    if len(last) % 2:
        last.append(jnp.zeros_like(last[0]))
    tiles += [jnp.concatenate(last[k : k + 2], axis=1) for k in range(0, len(last), 2)]
    return tiles


def unpacked(tiles, count, channels, index, tap):
    if tap < 2:
        tile = tiles[index]
        return tile[:, tap * channels : (tap + 1) * channels]
    tile = tiles[count + index // 2]
    side = index % 2
    return tile[:, side * channels : (side + 1) * channels]


def kernel(
    sizes,
    volume, w_first, w_second, cotangent,
    out, inp, first_out, second_out,
    vs, cs, hs, slope, pgs, w1f, w1t, w2f, w2t, cshift,
    part1, landed1, final1, part2, landed2, final2,
    raw_vol, raw_cot, raw_first, raw_second, vol, cot, w1p, w2g, w2o, load_sem,
    halo_send, halo_recv, fwd_send, fwd_recv, vfwd_send, vfwd_recv, gat_send, gat_recv,
    rs_send, rs_recv, ag_send, ag_recv,
):
    nb, nf, y_rows, width = sizes
    channels, z_cells = volume.shape[:2]
    own = cotangent.shape[0]
    half = channels // 2
    b = lax.axis_index("blocks")
    f = lax.axis_index("filt")
    mine = pl.ds(pl.multiple_of(f * own, own), own)
    core_half = pl.ds(pl.multiple_of(lax.rem(f, 2) * half, half), half)
    mate = f + 1 - 2 * lax.rem(f, 2)
    across = lax.rem(f + 2, nf)
    theirs = pl.ds(pl.multiple_of(across * own, own), own)

    barrier = pltpu.get_barrier_semaphore()
    for d in range(1, nf):
        pl.semaphore_signal(barrier, 1, device_id=(b, lax.rem(f + d, nf)), device_id_type=MESH)
    for d in range(1, nb):
        pl.semaphore_signal(barrier, 1, device_id=(lax.rem(b + d, nb), f), device_id_type=MESH)

    loads = [
        pltpu.make_async_copy(source, target, load_sem.at[k])
        for k, (source, target) in enumerate(
            ((cotangent, raw_cot), (w_first, raw_first), (volume, raw_vol), (w_second, raw_second))
        )
    ]
    for copy in loads:
        copy.start()

    hw = HALO * width
    body = y_rows * width
    low, mid, high = slice(0, hw), slice(hw, hw + body), slice(hw + body, 2 * hw + body)
    has_low, has_high = b > 0, b < nb - 1
    lands = (low, high)
    gives = (slice(body - hw, body), slice(0, hw))
    sends_if = (has_high, has_low)
    lands_if = (has_low, has_high)
    targets = (b + 1, b - 1)

    def remote(src, dst, send, recv, device):
        return pltpu.make_async_remote_copy(
            src_ref=src, dst_ref=dst, send_sem=send, recv_sem=recv, device_id=device, device_id_type=MESH
        )

    def halo(side):
        return (
            remote(vol.at[:, core_half, gives[side]], vs.at[:, core_half, lands[side]],
                   halo_send.at[side], halo_recv.at[side], (targets[side], f)),
            remote(cot.at[:, :, gives[side]], cs.at[:, mine, lands[side]],
                   halo_send.at[2 + side], halo_recv.at[2 + side], (targets[side], f)),
        )

    def forward_volume(side):
        ref = vs.at[:, core_half, lands[side]]
        return remote(ref, ref, vfwd_send.at[side], vfwd_recv.at[side], (b, mate))

    roles = ((mate, mine), (across, mine), (mate, theirs))

    def forward_cot(side, role):
        to, block = roles[role]
        ref = cs.at[:, block, lands[side]]
        slot = 2 * role + side
        return remote(ref, ref, fwd_send.at[slot], fwd_recv.at[slot], (b, to))

    def gather(k, role):
        to, block = roles[role]
        source = (w1p, cot, w2g)[k]
        ref = (w1f.at[:, block, :], cs.at[:, block, mid], w2f.at[:, :, block, :])[k]
        if role == 2:
            source = ref
        slot = 3 * role + k
        return remote(source, ref, gat_send.at[slot], gat_recv.at[slot], (b, to))

    def rows_first(raw, z):
        return jnp.transpose(raw[:, z].astype(jnp.float32), (1, 0, 2)).astype(raw.dtype)

    loads[0].wait()
    for z in range(z_cells):
        rows = rows_first(raw_cot, z)
        for y in range(y_rows):
            cot[z, :, y * width : (y + 1) * width] = rows[y]
    loads[1].wait()
    for c in range(3):
        w1p[c] = jnp.concatenate([raw_first[t, c] for t in range(3)], axis=1)
    loads[2].wait()
    for z in range(z_cells):
        rows = rows_first(raw_vol, z)
        for y in range(y_rows):
            vol[z, :, y * width : (y + 1) * width] = rows[y]
    loads[3].wait()
    for a in range(3):
        for t in range(3):
            w2g[a, t] = jnp.concatenate([raw_second[a, t, c] for c in range(3)], axis=1)
        for c in range(3):
            w2o[a, c * own : (c + 1) * own] = jnp.concatenate([raw_second[a, t, c] for t in range(3)], axis=1)
    vs[:, :, mid] = vol[...]
    cs[:, mine, mid] = cot[...]
    w1f[:, mine, :] = w1p[...]
    w2f[:, :, mine, :] = w2g[...]
    for side in (0, 1):
        @pl.when(jnp.logical_not(lands_if[side]))
        def _():
            vs[:, :, lands[side]] = jnp.zeros((z_cells, channels, hw), vs.dtype)
            cs[:, :, lands[side]] = jnp.zeros((z_cells, channels, hw), cs.dtype)
    pl.semaphore_wait(barrier, nf - 1 + nb - 1)
    for role in (1, 0):
        gather(0, role).start()
    for side in (0, 1):
        @pl.when(sends_if[side])
        def _():
            volume_copy, cot_copy = halo(side)
            cot_copy.start()
            volume_copy.start()
    for k in (1, 2):
        for role in (1, 0):
            gather(k, role).start()

    for z in range(z_cells):
        for y in range(y_rows):
            at = slice(y * width, (y + 1) * width)
            row = cot[z, :, at].astype(jnp.float32)
            for c in range(3):
                cshift[z, c * own : (c + 1) * own, at] = shifted(row, 2 * (c - 1)).astype(cshift.dtype)

    def pass_on(k):
        gather(k, 1).wait_recv()
        gather(k, 2).start()

    def complete(k):
        gather(k, 0).wait_recv()
        gather(k, 2).wait_recv()

    pass_on(0)
    complete(0)
    first_weight = w1f[...].reshape(3 * channels, w1f.shape[2])

    def first_layer(rows):
        for z in range(z_cells):
            product = dot(
                first_weight,
                taps_of(vs, z, [[y + t - 1 + HALO for y in rows] for t in range(3)], width),
            )
            for y, pre in zip(rows, gather_taps(product, width, channels, len(rows), (1, 0, -1))):
                at = slice((y + 2) * width, (y + 3) * width)
                sigma = 1.0 / (1.0 + jnp.exp(-pre))
                hs[z, :, at] = (pre * sigma).astype(hs.dtype)
                slope[z, :, at] = sigma * (1.0 + pre * (1.0 - sigma))

    inner = list(range(1, y_rows - 1))
    outer = [-2, -1, 0, y_rows - 1, y_rows, y_rows + 1]
    chunks = [inner[k : k + 2] for k in range(0, len(inner), 2)]
    first_layer(chunks[0])
    pass_on(1)
    for rows in chunks[1:2]:
        first_layer(rows)
    for side in (0, 1):
        @pl.when(lands_if[side])
        def _():
            volume_copy, cot_copy = halo(side)
            cot_copy.wait_recv()
            forward_cot(side, 1).start()
            forward_cot(side, 0).start()
    for rows in chunks[2:]:
        first_layer(rows)
    pass_on(2)
    for side in (0, 1):
        @pl.when(lands_if[side])
        def _():
            halo(side)[0].wait_recv()
            forward_volume(side).start()

    for c in range(3):
        w1t[c] = jnp.transpose(w1f[c])
    complete(1)
    complete(2)
    for a in range(3):
        w2t[a] = jnp.transpose(w2f[a].reshape(3 * channels, w2f.shape[3]))

    def hidden_grad(rows):
        for z in range(z_cells):
            product = None
            for a in range(3):
                at_z = z - 2 * (a - 1)
                if 0 <= at_z < z_cells:
                    term = dot(
                        w2t[a],
                        taps_of(cs, at_z, [[y - 2 * (t - 1) + HALO for y in rows] for t in range(3)], width),
                    )
                    product = term if product is None else product + term
            for y, value in zip(rows, gather_taps(product, width, channels, len(rows), (-2, 0, 2))):
                grad = value * slope[z, :, (y + 2) * width : (y + 3) * width]
                pgs[z, :, (y + 1) * width : (y + 2) * width] = grad.astype(pgs.dtype)

    inner_grad = list(range(2, y_rows - 2))
    outer_grad = [y for y in range(-1, y_rows + 1) if y not in inner_grad]
    for k in range(0, len(inner_grad), 2):
        hidden_grad(inner_grad[k : k + 2])

    for side in (0, 1):
        @pl.when(lands_if[side])
        def _():
            forward_volume(side).wait_recv()
            forward_cot(side, 1).wait_recv()
            forward_cot(side, 2).start()
    for k in range(0, len(outer), 2):
        first_layer(outer[k : k + 2])
    for side, at in ((0, slice(0, 2 * width)), (1, slice((y_rows + 2) * width, (y_rows + 4) * width))):
        @pl.when(jnp.logical_not(lands_if[side]))
        def _():
            hs[:, :, at] = jnp.zeros((z_cells, channels, 2 * width), hs.dtype)

    def hidden_taps(z, rows):
        return taps_of(hs, z, [[y + 2 * t for y in rows] for t in range(3)], width)

    factor = 1.0 / math.sqrt(z_cells * y_rows * nb * width)
    every = list(range(y_rows))
    lanes = 2 * channels

    def reduction(which, part, landed, final):
        chunk = part.shape[0] // nb

        def piece(index):
            return pl.ds(index * chunk, chunk)

        def scatter(d):
            to = lax.rem(b + d, nb)
            slot = which * nb + d
            return remote(part.at[piece(to)], landed.at[d], rs_send.at[slot], rs_recv.at[slot], (to, f))

        def spread(d):
            ref = final.at[piece(b)]
            slot = which * nb + d
            return remote(ref, ref, ag_send.at[slot], ag_recv.at[slot], (lax.rem(b + d, nb), f))

        def fill(blocks):
            tiles = packed(blocks, lanes)
            for k, tile in enumerate(tiles):
                part[k] = (tile * factor).astype(part.dtype)
            for k in range(len(tiles), part.shape[0]):
                part[k] = jnp.zeros(part.shape[1:], part.dtype)
            for d in range(1, nb):
                scatter(d).start()

        def turn():
            total = part[piece(b)].astype(jnp.float32)
            for d in range(1, nb):
                scatter(d).wait_recv()
                total = total + landed[d].astype(jnp.float32)
            final[piece(b)] = total.astype(final.dtype)
            for d in range(1, nb):
                spread(d).start()

        def finish():
            for d in range(1, nb):
                spread(d).wait_recv()

        def drain():
            for d in range(1, nb):
                scatter(d).wait_send()
                spread(d).wait_send()

        return fill, turn, finish, drain

    first_sum = reduction(0, part1, landed1, final1)
    second_sum = reduction(1, part2, landed2, final2)

    blocks = []
    for a in range(3):
        total = None
        for z in range(z_cells):
            at_z = z + 2 * (a - 1)
            if 0 <= at_z < z_cells:
                term = dot_cells(cshift[z], hidden_taps(at_z, every))
                total = term if total is None else total + term
        if total is None:
            total = jnp.zeros((3 * own, 3 * channels), jnp.float32)
        blocks += [total[c * own : (c + 1) * own] for c in range(3)]
    second_sum[0](blocks)

    for side in (0, 1):
        @pl.when(lands_if[side])
        def _():
            forward_cot(side, 0).wait_recv()
            forward_cot(side, 2).wait_recv()
    for k in range(0, len(outer_grad), 2):
        hidden_grad(outer_grad[k : k + 2])
    for side, at in ((0, slice(0, width)), (1, slice((y_rows + 1) * width, (y_rows + 2) * width))):
        @pl.when(jnp.logical_not(lands_if[side]))
        def _():
            pgs[:, :, at] = jnp.zeros((z_cells, channels, width), pgs.dtype)

    total = None
    for z in range(z_cells):
        columns = []
        for y in range(y_rows):
            row = pgs[z, mine, (y + 1) * width : (y + 2) * width].astype(jnp.float32)
            columns.append(
                jnp.concatenate([shifted(row, c - 1).astype(pgs.dtype) for c in range(3)], axis=0)
            )
        term = dot_cells(
            jnp.concatenate(columns, axis=1),
            taps_of(vs, z, [[y + t - 1 + HALO for y in every] for t in range(3)], width),
        )
        total = term if total is None else total + term
    first_sum[0]([total[c * own : (c + 1) * own] for c in range(3)])
    second_sum[1]()

    for z in range(z_cells):
        for k in range(0, y_rows, 2):
            product = None
            for a in range(3):
                at_z = z + 2 * (a - 1)
                if 0 <= at_z < z_cells:
                    term = dot(w2o[a], hidden_taps(at_z, every[k : k + 2]))
                    product = term if product is None else product + term
            for y, value in zip(every[k : k + 2], gather_taps(product, width, own, 2, (2, 0, -2))):
                out[z, :, y * width : (y + 1) * width] = value.astype(out.dtype)

    first_sum[1]()

    back_weight = jnp.concatenate(
        [
            jnp.concatenate(
                [w1t[c, pl.ds(pl.multiple_of(t * channels + f * own, own), own), :] for t in range(3)], axis=1
            )
            for c in range(3)
        ],
        axis=0,
    )
    for z in range(z_cells):
        for k in range(0, y_rows, 2):
            rows = every[k : k + 2]
            product = dot(back_weight, taps_of(pgs, z, [[y + 2 - t for y in rows] for t in range(3)], width))
            for y, value in zip(rows, gather_taps(product, width, own, 2, (-1, 0, 1))):
                inp[z, :, y * width : (y + 1) * width] = value.astype(inp.dtype)

    second_sum[2]()
    tiles = [final2[k].astype(jnp.float32) for k in range(14)]
    for a in range(3):
        for t in range(3):
            for c in range(3):
                second_out[a, t, c] = unpacked(tiles, 9, channels, 3 * a + c, t)
    first_sum[2]()
    tiles = [final1[k].astype(jnp.float32) for k in range(5)]
    for t in range(3):
        for c in range(3):
            first_out[t, c] = unpacked(tiles, 3, channels, c, t)

    for side in (0, 1):
        @pl.when(sends_if[side])
        def _():
            for copy in halo(side):
                copy.wait_send()

        @pl.when(lands_if[side])
        def _():
            forward_volume(side).wait_send()
            for role in range(3):
                forward_cot(side, role).wait_send()
    for role in range(3):
        for k in range(3):
            gather(k, role).wait_send()
    first_sum[3]()
    second_sum[3]()


def hand_out(out, inp, first, second, out_to, inp_to, first_to, second_to, sem):
    z_cells = out.shape[0]
    pairs = [(out.at[z], out_to.at[:, z]) for z in range(z_cells)]
    pairs += [(inp.at[z], inp_to.at[:, z]) for z in range(z_cells)]
    pairs += [(first, first_to), (second, second_to)]
    copies = [pltpu.make_async_copy(s, t, sem.at[k]) for k, (s, t) in enumerate(pairs)]
    for copy in copies:
        copy.start()
    for copy in copies:
        copy.wait()


def per_device(nb, nf, volume, w_first, w_second, cotangent):
    channels, z_cells, y_rows, width = volume.shape
    own = cotangent.shape[0]
    cells = y_rows * width
    tiles1, tiles2 = (-(-count // nb) * nb for count in (5, 14))
    tile = (own, 2 * channels)
    wide = (y_rows + 2 * HALO) * width
    bf16, f32 = jnp.bfloat16, jnp.float32
    dma = pltpu.SemaphoreType.DMA
    out, inp, first, second = pl.pallas_call(
        functools.partial(kernel, (nb, nf, y_rows, width)),
        out_shape=(
            jax.ShapeDtypeStruct((z_cells, own, cells), bf16),
            jax.ShapeDtypeStruct((z_cells, own, cells), bf16),
            jax.ShapeDtypeStruct((3, 3, own, channels), f32),
            jax.ShapeDtypeStruct((3, 3, 3, own, channels), f32),
        ),
        in_specs=[pl.BlockSpec(memory_space=pltpu.HBM)] * 4,
        out_specs=(pl.BlockSpec(memory_space=pltpu.VMEM),) * 4,
        scratch_shapes=[
            pltpu.VMEM((z_cells, channels, wide), bf16),
            pltpu.VMEM((z_cells, channels, wide), bf16),
            pltpu.VMEM((z_cells, channels, (y_rows + 4) * width), bf16),
            pltpu.VMEM((z_cells, channels, (y_rows + 4) * width), f32),
            pltpu.VMEM((z_cells, channels, (y_rows + 2) * width), bf16),
            pltpu.VMEM((3, channels, 3 * channels), bf16),
            pltpu.VMEM((3, 3 * channels, channels), bf16),
            pltpu.VMEM((3, 3, channels, 3 * channels), bf16),
            pltpu.VMEM((3, 3 * channels, 3 * channels), bf16),
            pltpu.VMEM((z_cells, 3 * own, cells), bf16),
            pltpu.VMEM((tiles1,) + tile, bf16),
            pltpu.VMEM((nb, tiles1 // nb) + tile, bf16),
            pltpu.VMEM((tiles1,) + tile, bf16),
            pltpu.VMEM((tiles2,) + tile, bf16),
            pltpu.VMEM((nb, tiles2 // nb) + tile, bf16),
            pltpu.VMEM((tiles2,) + tile, bf16),
            pltpu.VMEM(volume.shape, bf16),
            pltpu.VMEM(cotangent.shape, bf16),
            pltpu.VMEM(w_first.shape, bf16),
            pltpu.VMEM(w_second.shape, bf16),
            pltpu.VMEM((z_cells, channels, cells), bf16),
            pltpu.VMEM((z_cells, own, cells), bf16),
            pltpu.VMEM((3, own, 3 * channels), bf16),
            pltpu.VMEM((3, 3, own, 3 * channels), bf16),
            pltpu.VMEM((3, 3 * own, 3 * channels), bf16),
            dma((4,)),
            dma((4,)), dma((4,)), dma((6,)), dma((6,)), dma((2,)), dma((2,)), dma((9,)), dma((9,)),
            dma((2 * nb,)), dma((2 * nb,)), dma((2 * nb,)), dma((2 * nb,)),
        ],
        compiler_params=pltpu.CompilerParams(
            collective_id=0, has_side_effects=True, vmem_limit_bytes=40 * 1024 * 1024
        ),
    )(volume, w_first, w_second, cotangent)
    planes = (z_cells, own, y_rows, width)
    output, input_grad, first, second = pl.pallas_call(
        hand_out,
        out_shape=(
            jax.ShapeDtypeStruct(cotangent.shape, bf16),
            jax.ShapeDtypeStruct(cotangent.shape, bf16),
            jax.ShapeDtypeStruct(first.shape, f32),
            jax.ShapeDtypeStruct(second.shape, f32),
        ),
        in_specs=[pl.BlockSpec(memory_space=pltpu.VMEM)] * 4,
        out_specs=(pl.BlockSpec(memory_space=pltpu.HBM),) * 4,
        scratch_shapes=[dma((2 * z_cells + 2,))],
    )(out.reshape(planes), inp.reshape(planes), first, second)
    return (output, input_grad, first, second)


def solution(mesh):
    return jax.shard_map(
        functools.partial(per_device, mesh.shape["blocks"], mesh.shape["filt"]),
        mesh=mesh,
        in_specs=(
            P(None, None, "blocks", None),
            P(None, None, "filt", None),
            P(None, None, None, "filt", None),
            P("filt", None, "blocks", None),
        ),
        out_specs=(
            P("filt", None, "blocks", None),
            P("filt", None, "blocks", None),
            P(None, None, "filt", None),
            P(None, None, None, "filt", None),
        ),
        check_vma=False,
    )
```

```python
import functools
import math

import jax
import jax.numpy as jnp
from jax import lax
from jax.experimental import pallas as pl
from jax.experimental.pallas import tpu as pltpu
from jax.sharding import PartitionSpec as P

HALO = 3
MESH = pl.DeviceIdType.MESH


def shifted(row, amount):
    if amount == 0:
        return row
    width = row.shape[1]
    lane = lax.broadcasted_iota(jnp.int32, row.shape, 1)
    moved = pltpu.roll(row, amount % width, 1)
    keep = lane >= amount if amount > 0 else lane < width + amount
    return jnp.where(keep, moved, 0.0)


def rows_of(ref, z, rows, width):
    pieces = []
    start = 0
    while start < len(rows):
        stop = start + 1
        while stop < len(rows) and rows[stop] == rows[stop - 1] + 1:
            stop += 1
        pieces.append(ref[z, :, rows[start] * width : (rows[stop - 1] + 1) * width])
        start = stop
    return pieces[0] if len(pieces) == 1 else jnp.concatenate(pieces, axis=1)


def taps_of(ref, z, row_lists, width):
    return jnp.concatenate([rows_of(ref, z, rows, width) for rows in row_lists], axis=0)


def gather_taps(product, width, channels, count, amounts):
    out = []
    for r in range(count):
        total = None
        for c in range(3):
            part = product[c * channels : (c + 1) * channels, r * width : (r + 1) * width]
            part = shifted(part, amounts[c])
            total = part if total is None else total + part
        out.append(total)
    return out


def dot(a, b):
    return jnp.dot(a, b, preferred_element_type=jnp.float32)


def dot_cells(a, b):
    return lax.dot_general(a, b, (((1,), (1,)), ((), ())), preferred_element_type=jnp.float32)


def packed(blocks, lanes):
    tiles = [block[:, :lanes] for block in blocks]
    last = [block[:, lanes:] for block in blocks]
    if len(last) % 2:
        last.append(jnp.zeros_like(last[0]))
    tiles += [jnp.concatenate(last[k : k + 2], axis=1) for k in range(0, len(last), 2)]
    return tiles


def unpacked(tiles, count, channels, index, tap):
    if tap < 2:
        tile = tiles[index]
        return tile[:, tap * channels : (tap + 1) * channels]
    tile = tiles[count + index // 2]
    side = index % 2
    return tile[:, side * channels : (side + 1) * channels]


def kernel(
    sizes,
    volume, w_first, w_second, cotangent,
    out, inp, first_out, second_out,
    vs, cs, hs, slope, pgs, w1f, w1t, w2f, w2t, cshift,
    part1, landed1, final1, part2, landed2, final2,
    raw_vol, raw_cot, raw_first, raw_second, vol, cot, w1p, w2g, w2o, load_sem,
    halo_send, halo_recv, fwd_send, fwd_recv, vfwd_send, vfwd_recv, gat_send, gat_recv,
    rs_send, rs_recv, ag_send, ag_recv,
):
    nb, nf, y_rows, width = sizes
    channels, z_cells = volume.shape[:2]
    own = cotangent.shape[0]
    half = channels // 2
    b = lax.axis_index("blocks")
    f = lax.axis_index("filt")
    mine = pl.ds(pl.multiple_of(f * own, own), own)
    core_half = pl.ds(pl.multiple_of(lax.rem(f, 2) * half, half), half)
    mate = f + 1 - 2 * lax.rem(f, 2)
    across = lax.rem(f + 2, nf)
    theirs = pl.ds(pl.multiple_of(across * own, own), own)

    barrier = pltpu.get_barrier_semaphore()
    for d in range(1, nf):
        pl.semaphore_signal(barrier, 1, device_id=(b, lax.rem(f + d, nf)), device_id_type=MESH)
    for d in range(1, nb):
        pl.semaphore_signal(barrier, 1, device_id=(lax.rem(b + d, nb), f), device_id_type=MESH)

    loads = [
        pltpu.make_async_copy(source, target, load_sem.at[k])
        for k, (source, target) in enumerate(
            ((cotangent, raw_cot), (w_first, raw_first), (volume, raw_vol), (w_second, raw_second))
        )
    ]
    for copy in loads:
        copy.start()

    hw = HALO * width
    body = y_rows * width
    low, mid, high = slice(0, hw), slice(hw, hw + body), slice(hw + body, 2 * hw + body)
    has_low, has_high = b > 0, b < nb - 1
    lands = (low, high)
    gives = (slice(body - hw, body), slice(0, hw))
    sends_if = (has_high, has_low)
    lands_if = (has_low, has_high)
    targets = (b + 1, b - 1)

    def remote(src, dst, send, recv, device):
        return pltpu.make_async_remote_copy(
            src_ref=src, dst_ref=dst, send_sem=send, recv_sem=recv, device_id=device, device_id_type=MESH
        )

    def halo(side):
        return (
            remote(vol.at[:, core_half, gives[side]], vs.at[:, core_half, lands[side]],
                   halo_send.at[side], halo_recv.at[side], (targets[side], f)),
            remote(cot.at[:, :, gives[side]], cs.at[:, mine, lands[side]],
                   halo_send.at[2 + side], halo_recv.at[2 + side], (targets[side], f)),
        )

    def forward_volume(side):
        ref = vs.at[:, core_half, lands[side]]
        return remote(ref, ref, vfwd_send.at[side], vfwd_recv.at[side], (b, mate))

    roles = ((mate, mine), (across, mine), (mate, theirs))

    def forward_cot(side, role):
        to, block = roles[role]
        ref = cs.at[:, block, lands[side]]
        slot = 2 * role + side
        return remote(ref, ref, fwd_send.at[slot], fwd_recv.at[slot], (b, to))

    def gather(k, role):
        to, block = roles[role]
        source = (w1p, cot, w2g)[k]
        ref = (w1f.at[:, block, :], cs.at[:, block, mid], w2f.at[:, :, block, :])[k]
        if role == 2:
            source = ref
        slot = 3 * role + k
        return remote(source, ref, gat_send.at[slot], gat_recv.at[slot], (b, to))

    def rows_first(raw, z):
        return jnp.transpose(raw[:, z].astype(jnp.float32), (1, 0, 2)).astype(raw.dtype)

    loads[0].wait()
    for z in range(z_cells):
        rows = rows_first(raw_cot, z)
        for y in range(y_rows):
            cot[z, :, y * width : (y + 1) * width] = rows[y]
    loads[1].wait()
    for c in range(3):
        w1p[c] = jnp.concatenate([raw_first[t, c] for t in range(3)], axis=1)
    loads[2].wait()
    for z in range(z_cells):
        rows = rows_first(raw_vol, z)
        for y in range(y_rows):
            vol[z, :, y * width : (y + 1) * width] = rows[y]
    loads[3].wait()
    for a in range(3):
        for t in range(3):
            w2g[a, t] = jnp.concatenate([raw_second[a, t, c] for c in range(3)], axis=1)
        for c in range(3):
            w2o[a, c * own : (c + 1) * own] = jnp.concatenate([raw_second[a, t, c] for t in range(3)], axis=1)
    vs[:, :, mid] = vol[...]
    cs[:, mine, mid] = cot[...]
    w1f[:, mine, :] = w1p[...]
    w2f[:, :, mine, :] = w2g[...]
    for side in (0, 1):
        @pl.when(jnp.logical_not(lands_if[side]))
        def _():
            vs[:, :, lands[side]] = jnp.zeros((z_cells, channels, hw), vs.dtype)
            cs[:, :, lands[side]] = jnp.zeros((z_cells, channels, hw), cs.dtype)
    pl.semaphore_wait(barrier, nf - 1 + nb - 1)
    for role in (1, 0):
        gather(0, role).start()
    for side in (0, 1):
        @pl.when(sends_if[side])
        def _():
            volume_copy, cot_copy = halo(side)
            cot_copy.start()
            volume_copy.start()
    for k in (1, 2):
        for role in (1, 0):
            gather(k, role).start()

    for z in range(z_cells):
        for y in range(y_rows):
            at = slice(y * width, (y + 1) * width)
            row = cot[z, :, at].astype(jnp.float32)
            for c in range(3):
                cshift[z, c * own : (c + 1) * own, at] = shifted(row, 2 * (c - 1)).astype(cshift.dtype)

    def pass_on(k):
        gather(k, 1).wait_recv()
        gather(k, 2).start()

    def complete(k):
        gather(k, 0).wait_recv()
        gather(k, 2).wait_recv()

    pass_on(0)
    complete(0)
    first_weight = w1f[...].reshape(3 * channels, w1f.shape[2])

    def first_layer(rows):
        for z in range(z_cells):
            product = dot(
                first_weight,
                taps_of(vs, z, [[y + t - 1 + HALO for y in rows] for t in range(3)], width),
            )
            for y, pre in zip(rows, gather_taps(product, width, channels, len(rows), (1, 0, -1))):
                at = slice((y + 2) * width, (y + 3) * width)
                sigma = 1.0 / (1.0 + jnp.exp(-pre))
                hs[z, :, at] = (pre * sigma).astype(hs.dtype)
                slope[z, :, at] = sigma * (1.0 + pre * (1.0 - sigma))

    inner = list(range(1, y_rows - 1))
    outer = [-2, -1, 0, y_rows - 1, y_rows, y_rows + 1]
    chunks = [inner[k : k + 2] for k in range(0, len(inner), 2)]
    first_layer(chunks[0])
    pass_on(1)
    for rows in chunks[1:2]:
        first_layer(rows)
    for side in (0, 1):
        @pl.when(lands_if[side])
        def _():
            volume_copy, cot_copy = halo(side)
            cot_copy.wait_recv()
            forward_cot(side, 1).start()
            forward_cot(side, 0).start()
    for rows in chunks[2:]:
        first_layer(rows)
    pass_on(2)
    for side in (0, 1):
        @pl.when(lands_if[side])
        def _():
            halo(side)[0].wait_recv()
            forward_volume(side).start()

    for c in range(3):
        w1t[c] = jnp.transpose(w1f[c])
    complete(1)
    complete(2)
    for a in range(3):
        w2t[a] = jnp.transpose(w2f[a].reshape(3 * channels, w2f.shape[3]))

    def hidden_grad(rows):
        for z in range(z_cells):
            product = None
            for a in range(3):
                at_z = z - 2 * (a - 1)
                if 0 <= at_z < z_cells:
                    term = dot(
                        w2t[a],
                        taps_of(cs, at_z, [[y - 2 * (t - 1) + HALO for y in rows] for t in range(3)], width),
                    )
                    product = term if product is None else product + term
            for y, value in zip(rows, gather_taps(product, width, channels, len(rows), (-2, 0, 2))):
                grad = value * slope[z, :, (y + 2) * width : (y + 3) * width]
                pgs[z, :, (y + 1) * width : (y + 2) * width] = grad.astype(pgs.dtype)

    inner_grad = list(range(2, y_rows - 2))
    outer_grad = [y for y in range(-1, y_rows + 1) if y not in inner_grad]
    for k in range(0, len(inner_grad), 2):
        hidden_grad(inner_grad[k : k + 2])

    for side in (0, 1):
        @pl.when(lands_if[side])
        def _():
            forward_volume(side).wait_recv()
            forward_cot(side, 1).wait_recv()
            forward_cot(side, 2).start()
    for k in range(0, len(outer), 2):
        first_layer(outer[k : k + 2])
    for side, at in ((0, slice(0, 2 * width)), (1, slice((y_rows + 2) * width, (y_rows + 4) * width))):
        @pl.when(jnp.logical_not(lands_if[side]))
        def _():
            hs[:, :, at] = jnp.zeros((z_cells, channels, 2 * width), hs.dtype)

    def hidden_taps(z, rows):
        return taps_of(hs, z, [[y + 2 * t for y in rows] for t in range(3)], width)

    factor = 1.0 / math.sqrt(z_cells * y_rows * nb * width)
    every = list(range(y_rows))
    lanes = 2 * channels

    def reduction(which, part, landed, final):
        chunk = part.shape[0] // nb

        def piece(index):
            return pl.ds(index * chunk, chunk)

        def scatter(d):
            to = lax.rem(b + d, nb)
            slot = which * nb + d
            return remote(part.at[piece(to)], landed.at[d], rs_send.at[slot], rs_recv.at[slot], (to, f))

        def spread(d):
            ref = final.at[piece(b)]
            slot = which * nb + d
            return remote(ref, ref, ag_send.at[slot], ag_recv.at[slot], (lax.rem(b + d, nb), f))

        def fill(blocks):
            tiles = packed(blocks, lanes)
            for k, tile in enumerate(tiles):
                part[k] = (tile * factor).astype(part.dtype)
            for k in range(len(tiles), part.shape[0]):
                part[k] = jnp.zeros(part.shape[1:], part.dtype)
            for d in range(1, nb):
                scatter(d).start()

        def turn():
            total = part[piece(b)].astype(jnp.float32)
            for d in range(1, nb):
                scatter(d).wait_recv()
                total = total + landed[d].astype(jnp.float32)
            final[piece(b)] = total.astype(final.dtype)
            for d in range(1, nb):
                spread(d).start()

        def finish():
            for d in range(1, nb):
                spread(d).wait_recv()

        def drain():
            for d in range(1, nb):
                scatter(d).wait_send()
                spread(d).wait_send()

        return fill, turn, finish, drain

    first_sum = reduction(0, part1, landed1, final1)
    second_sum = reduction(1, part2, landed2, final2)

    blocks = []
    for a in range(3):
        total = None
        for z in range(z_cells):
            at_z = z + 2 * (a - 1)
            if 0 <= at_z < z_cells:
                term = dot_cells(cshift[z], hidden_taps(at_z, every))
                total = term if total is None else total + term
        if total is None:
            total = jnp.zeros((3 * own, 3 * channels), jnp.float32)
        blocks += [total[c * own : (c + 1) * own] for c in range(3)]
    second_sum[0](blocks)

    for side in (0, 1):
        @pl.when(lands_if[side])
        def _():
            forward_cot(side, 0).wait_recv()
            forward_cot(side, 2).wait_recv()
    for k in range(0, len(outer_grad), 2):
        hidden_grad(outer_grad[k : k + 2])
    for side, at in ((0, slice(0, width)), (1, slice((y_rows + 1) * width, (y_rows + 2) * width))):
        @pl.when(jnp.logical_not(lands_if[side]))
        def _():
            pgs[:, :, at] = jnp.zeros((z_cells, channels, width), pgs.dtype)

    total = None
    for z in range(z_cells):
        columns = []
        for y in range(y_rows):
            row = pgs[z, mine, (y + 1) * width : (y + 2) * width].astype(jnp.float32)
            columns.append(
                jnp.concatenate([shifted(row, c - 1).astype(pgs.dtype) for c in range(3)], axis=0)
            )
        term = dot_cells(
            jnp.concatenate(columns, axis=1),
            taps_of(vs, z, [[y + t - 1 + HALO for y in every] for t in range(3)], width),
        )
        total = term if total is None else total + term
    first_sum[0]([total[c * own : (c + 1) * own] for c in range(3)])
    second_sum[1]()

    for z in range(z_cells):
        for k in range(0, y_rows, 2):
            product = None
            for a in range(3):
                at_z = z + 2 * (a - 1)
                if 0 <= at_z < z_cells:
                    term = dot(w2o[a], hidden_taps(at_z, every[k : k + 2]))
                    product = term if product is None else product + term
            for y, value in zip(every[k : k + 2], gather_taps(product, width, own, 2, (2, 0, -2))):
                out[z, :, y * width : (y + 1) * width] = value.astype(out.dtype)

    first_sum[1]()

    back_weight = jnp.concatenate(
        [
            jnp.concatenate(
                [w1t[c, pl.ds(pl.multiple_of(t * channels + f * own, own), own), :] for t in range(3)], axis=1
            )
            for c in range(3)
        ],
        axis=0,
    )
    for z in range(z_cells):
        for k in range(0, y_rows, 2):
            rows = every[k : k + 2]
            product = dot(back_weight, taps_of(pgs, z, [[y + 2 - t for y in rows] for t in range(3)], width))
            for y, value in zip(rows, gather_taps(product, width, own, 2, (-1, 0, 1))):
                inp[z, :, y * width : (y + 1) * width] = value.astype(inp.dtype)

    second_sum[2]()
    tiles = [final2[k].astype(jnp.float32) for k in range(14)]
    for a in range(3):
        for t in range(3):
            for c in range(3):
                second_out[a, t, c] = unpacked(tiles, 9, channels, 3 * a + c, t)
    first_sum[2]()
    tiles = [final1[k].astype(jnp.float32) for k in range(5)]
    for t in range(3):
        for c in range(3):
            first_out[t, c] = unpacked(tiles, 3, channels, c, t)

    for side in (0, 1):
        @pl.when(sends_if[side])
        def _():
            for copy in halo(side):
                copy.wait_send()

        @pl.when(lands_if[side])
        def _():
            forward_volume(side).wait_send()
            for role in range(3):
                forward_cot(side, role).wait_send()
    for role in range(3):
        for k in range(3):
            gather(k, role).wait_send()
    first_sum[3]()
    second_sum[3]()


def per_device(nb, nf, volume, w_first, w_second, cotangent):
    channels, z_cells, y_rows, width = volume.shape
    own = cotangent.shape[0]
    cells = y_rows * width
    tiles1, tiles2 = (-(-count // nb) * nb for count in (5, 14))
    tile = (own, 2 * channels)
    wide = (y_rows + 2 * HALO) * width
    bf16, f32 = jnp.bfloat16, jnp.float32
    dma = pltpu.SemaphoreType.DMA
    out, inp, first, second = pl.pallas_call(
        functools.partial(kernel, (nb, nf, y_rows, width)),
        out_shape=(
            jax.ShapeDtypeStruct((z_cells, own, cells), bf16),
            jax.ShapeDtypeStruct((z_cells, own, cells), bf16),
            jax.ShapeDtypeStruct((3, 3, own, channels), f32),
            jax.ShapeDtypeStruct((3, 3, 3, own, channels), f32),
        ),
        in_specs=[pl.BlockSpec(memory_space=pltpu.HBM)] * 4,
        out_specs=(pl.BlockSpec(memory_space=pltpu.VMEM),) * 4,
        scratch_shapes=[
            pltpu.VMEM((z_cells, channels, wide), bf16),
            pltpu.VMEM((z_cells, channels, wide), bf16),
            pltpu.VMEM((z_cells, channels, (y_rows + 4) * width), bf16),
            pltpu.VMEM((z_cells, channels, (y_rows + 4) * width), f32),
            pltpu.VMEM((z_cells, channels, (y_rows + 2) * width), bf16),
            pltpu.VMEM((3, channels, 3 * channels), bf16),
            pltpu.VMEM((3, 3 * channels, channels), bf16),
            pltpu.VMEM((3, 3, channels, 3 * channels), bf16),
            pltpu.VMEM((3, 3 * channels, 3 * channels), bf16),
            pltpu.VMEM((z_cells, 3 * own, cells), bf16),
            pltpu.VMEM((tiles1,) + tile, bf16),
            pltpu.VMEM((nb, tiles1 // nb) + tile, bf16),
            pltpu.VMEM((tiles1,) + tile, bf16),
            pltpu.VMEM((tiles2,) + tile, bf16),
            pltpu.VMEM((nb, tiles2 // nb) + tile, bf16),
            pltpu.VMEM((tiles2,) + tile, bf16),
            pltpu.VMEM(volume.shape, bf16),
            pltpu.VMEM(cotangent.shape, bf16),
            pltpu.VMEM(w_first.shape, bf16),
            pltpu.VMEM(w_second.shape, bf16),
            pltpu.VMEM((z_cells, channels, cells), bf16),
            pltpu.VMEM((z_cells, own, cells), bf16),
            pltpu.VMEM((3, own, 3 * channels), bf16),
            pltpu.VMEM((3, 3, own, 3 * channels), bf16),
            pltpu.VMEM((3, 3 * own, 3 * channels), bf16),
            dma((4,)),
            dma((4,)), dma((4,)), dma((6,)), dma((6,)), dma((2,)), dma((2,)), dma((9,)), dma((9,)),
            dma((2 * nb,)), dma((2 * nb,)), dma((2 * nb,)), dma((2 * nb,)),
        ],
        compiler_params=pltpu.CompilerParams(
            collective_id=0, has_side_effects=True, vmem_limit_bytes=64 * 1024 * 1024 - 512 * 1024
        ),
    )(volume, w_first, w_second, cotangent)
    output = out.reshape(z_cells, own, y_rows, width).transpose(1, 0, 2, 3)
    input_grad = inp.reshape(z_cells, own, y_rows, width).transpose(1, 0, 2, 3)
    return (output, input_grad, first, second)


def solution(mesh):
    return jax.shard_map(
        functools.partial(per_device, mesh.shape["blocks"], mesh.shape["filt"]),
        mesh=mesh,
        in_specs=(
            P(None, None, "blocks", None),
            P(None, None, "filt", None),
            P(None, None, None, "filt", None),
            P("filt", None, "blocks", None),
        ),
        out_specs=(
            P("filt", None, "blocks", None),
            P("filt", None, "blocks", None),
            P(None, None, "filt", None),
            P(None, None, None, "filt", None),
        ),
        check_vma=False,
    )
```
